32 devices in a mesh: rows: 16 (over z, x, core), vecs: 2 (over y).
Axes of the slice: x: 2, y: 2, z: 4, core: 2. Of those that a mesh axis runs over, the one named last changes fastest.
Arguments:
- tiles: bfloat16 [64, 6, 128, 128], P('rows'), as said below
- columns: int32 [64, 6], P('rows'), may hold values from 0 to 63, as said below
- start_vectors: float32 [1024, 8192], P('vecs', 'rows'), may hold values from -6 to 6
Outputs:
- basis: float32 [1024, 8192], P('vecs', 'rows')
The draws below stay inside these ranges and needn't reach their ends.
Inputs may be any that keep to these rules, and one draw needn't show every extreme that they name: `columns`: the 6 column blocks of row block b are distinct; they are b, b - 1, b + 1 and three of b - 3, b - 2, b + 2, b + 3, all modulo 64, the first three in this order. The pattern is symmetric: block c is among those of row block b exactly when b is among those of row block c. `tiles`: H is symmetric: the tile of row block b at column block c is the transpose of the tile of row block c at column block b.
All inputs are finite; a program needn't handle non-finite values.
Results may differ from the reference program's by a relative error of at most 0.0003.
Values sent between devices are 32-bit elements; how exact they have to be, the bound alone decides.
No kernel may reach another device: no remote copies, remote signals or barrier semaphores. Data moves between devices by JAX's collectives and lax.ppermute only.
A program may use at most 64 MiB of HBM per device.

```python
import jax
import jax.numpy as jnp
from jax import lax

M = 1024
BS = 128
STEPS = 4
NBLK = 64
NROW = 8192


def block_offsets(key):
    pattern_key = jax.random.fold_in(key, 7)
    phase_key, order_key = jax.random.split(pattern_key)
    phase = jax.random.randint(phase_key, (), 0, 4, dtype=jnp.int32)
    base = jnp.arange(NBLK, dtype=jnp.int32)
    position = jnp.mod(base - phase, 4)
    missing = jnp.where(position < 2, 2, -2).astype(jnp.int32)
    farther = jnp.array([-3, -2, 2, 3], dtype=jnp.int32)
    keep = farther[None, :] != missing[:, None]
    ranks = jnp.where(keep, jnp.arange(4, dtype=jnp.int32)[None, :], 4)
    chosen = jnp.argsort(ranks, axis=1, stable=True)[:, :3]
    kept = farther[chosen]
    row_keys = jax.random.split(order_key, NBLK)

    def shuffle(single, values):
        return jax.random.permutation(single, values)
    kept = jax.vmap(shuffle)(row_keys, kept)
    nearby = jnp.broadcast_to(jnp.array([0, -1, 1], dtype=jnp.int32), (NBLK, 3))
    return jnp.concatenate([nearby, kept], axis=1).astype(jnp.int32)


def draw_columns(key, part):
    offsets = block_offsets(key)
    base = jnp.arange(NBLK, dtype=jnp.int32)[:, None]
    return jnp.mod(base + offsets, NBLK).astype(jnp.int32)


def draw_tiles(key, part):
    offsets = block_offsets(key)
    tile_key = jax.random.fold_in(key, 11)
    spread = (24.0 * BS) ** (-0.5)
    edges = jax.random.normal(tile_key, (NBLK, 4, BS, BS), dtype=jnp.float32) * spread
    base = jnp.arange(NBLK, dtype=jnp.int32)[:, None]
    source = jnp.mod(jnp.where(offsets >= 0, base, base + offsets), NBLK).astype(jnp.int32)
    distance = jnp.abs(offsets).astype(jnp.int32)
    picked = edges[source, distance]
    flipped = jnp.swapaxes(picked, 2, 3)
    upper = jnp.where((offsets > 0)[:, :, None, None], picked, flipped)
    symmetric = (picked + flipped) * 0.5 ** 0.5
    result = jnp.where((offsets == 0)[:, :, None, None], symmetric, upper)
    return result.astype(jnp.bfloat16)


def shard_levels(rng, dims, cuts, smallest, top_value):
    def one(dim, blocks):
        draws = jax.random.uniform(jax.random.fold_in(jax.random.fold_in(rng, 6), dim), (blocks,), jnp.float32, smallest / len(cuts), top_value / len(cuts))
        return jnp.repeat(jnp.exp(draws), dims[dim] // blocks).reshape((-1,) + (1,) * (len(dims) - dim - 1))

    level = one(*cuts[0])
    for cut in cuts[1:]:
        level = level * one(*cut)
    return level


def noise(key, extent, width, most, cuts=(), kind=jnp.bfloat16):
    values = jax.random.normal(key, extent, jnp.float32) * width
    if len(cuts) > 0:
        values = shard_levels(key, extent, cuts, -0.22, 0.18) * values
    return jnp.clip(values, min=-most, max=most).astype(kind)


def setup_inputs(seed: int = 0) -> dict:
    arg_keys = jax.random.split(jax.random.key(seed), 4)
    tiles = draw_tiles(jax.random.fold_in(arg_keys[3], 71), 0)
    columns = draw_columns(jax.random.fold_in(arg_keys[3], 71), 0)
    start_vectors = noise(arg_keys[2], (M, NROW), 1.0, 6.0, ((0, 2), (1, 16)), jnp.float32)
    return dict(tiles=tiles, columns=columns, start_vectors=start_vectors)


def operate(field, tiles32, columns):
    blocked = field.reshape(M, NBLK, BS)

    def one_block(index):
        picked = jnp.take(blocked, columns[index], axis=1)
        return jnp.einsum('mtj,tij->mi', picked, tiles32[index], precision=lax.Precision.HIGHEST)
    outs = lax.map(one_block, jnp.arange(NBLK, dtype=jnp.int32))
    return jnp.transpose(outs, (1, 0, 2)).reshape(M, NBLK * BS)

def reference(tiles, columns, start_vectors):
    tiles32 = tiles.astype(jnp.float32)
    previous = start_vectors
    current = operate(start_vectors, tiles32, columns)
    for step in range(STEPS - 1):
        following = 2.0 * operate(current, tiles32, columns) - previous
        previous = current
        current = following
    gram = jnp.einsum('mn,kn->mk', current, current, precision=lax.Precision.HIGHEST)
    factor = jnp.linalg.cholesky(gram)
    solved = lax.linalg.triangular_solve(factor, current, left_side=True, lower=True)
    return solved * jnp.sqrt(jnp.float32(NBLK * BS))
```

```python
import functools

import jax
import jax.numpy as jnp
from jax import lax
from jax.experimental import pallas as pl
from jax.experimental.pallas import tpu as pltpu
from jax.sharding import PartitionSpec as P

BS = 128
HB = 3
STEPS = 4
NB = 128
SUB = 8
CHUNKS = 2
NT = (((1,), (1,)), ((), ()))
NN = (((1,), (0,)), ((), ()))
SCALARS = pl.BlockSpec(memory_space=pltpu.SMEM)
WHOLE = pl.BlockSpec(memory_space=pltpu.VMEM)
AFAR = pl.BlockSpec(memory_space=pltpu.HBM)
ROOMY = pltpu.CompilerParams(vmem_limit_bytes=28 * 2 ** 20)


def split(x):
    high = x.astype(jnp.bfloat16)
    return high, (x - high.astype(jnp.float32)).astype(jnp.bfloat16)


def dot3(a, b, dims):
    def dot(x, y):
        return lax.dot_general(x, y, dims, preferred_element_type=jnp.float32)

    return dot(a[0], b[0]) + (dot(a[0], b[1]) + dot(a[1], b[0]))


def band_kernel(slots_ref, tiles_ref, band_ref):
    band_ref[...] = jnp.zeros_like(band_ref)
    for b in range(tiles_ref.shape[0]):
        for t in range(tiles_ref.shape[1]):
            start = pl.multiple_of(slots_ref[b, t] * BS, BS)
            flipped = tiles_ref[b, t].astype(jnp.float32).T
            band_ref[pl.ds(start, BS), b * BS:(b + 1) * BS] = flipped.astype(jnp.bfloat16)


def band_matrix(tiles, slots):
    blocks = tiles.shape[0]
    return pl.pallas_call(
        band_kernel,
        out_shape=jax.ShapeDtypeStruct(((blocks + 2 * HB) * BS, blocks * BS), jnp.bfloat16),
        in_specs=[SCALARS, WHOLE],
        out_specs=WHOLE,
        compiler_params=ROOMY,
        name="band_matrix",
    )(slots, tiles)


def step_kernel(has_previous, has_edges, *refs):
    before_ref, current_ref, after_ref, band_ref = refs[:4]
    outs = refs[4 + has_previous:]
    parts = [ref[...] for ref in (before_ref, current_ref, after_ref)]
    highs, lows = zip(*[split(part) for part in parts])
    high, low = jnp.concatenate(highs, axis=1), jnp.concatenate(lows, axis=1)
    columns = current_ref.shape[1]
    blocks = columns // BS
    halo = HB * BS
    for b in range(0, blocks, 2):
        end = min(b + 2, blocks)
        here = slice(b * BS, end * BS)
        depth = slice(b * BS, (end + 2 * HB) * BS)
        band = band_ref[depth, here]

        def dot(x):
            return jnp.dot(x[:, depth], band, preferred_element_type=jnp.float32)

        result = dot(high) + dot(low)
        if has_previous:
            result = 2.0 * result - refs[4][:, here]
        outs[0][:, here] = result
    if has_edges:
        outs[1][...] = outs[0][:, columns - halo:]
        outs[2][...] = outs[0][:, :halo]


def filter_step(halos, current, band, previous, has_edges):
    before, after = halos
    width, columns = current.shape
    f32 = jnp.float32
    edge = jax.ShapeDtypeStruct((width, HB * BS), f32)
    shapes = (jax.ShapeDtypeStruct((width, columns), f32),) + (edge, edge) * has_edges
    operands = (before, current, after, band) + ((previous,) if previous is not None else ())
    return pl.pallas_call(
        functools.partial(step_kernel, previous is not None, has_edges),
        out_shape=shapes,
        in_specs=[WHOLE] * len(operands),
        out_specs=(WHOLE,) * len(shapes),
        compiler_params=ROOMY,
        cost_estimate=pl.CostEstimate(
            flops=4 * width * columns * (2 + 2 * HB) * BS,
            bytes_accessed=4 * width * columns * 6,
            transcendentals=0,
        ),
        name="filter_step",
    )(*operands)


def exchange_edges(last, first):
    devices = lax.axis_size("rows")
    up = [(i, (i + 1) % devices) for i in range(devices)]
    down = [(j, i) for i, j in up]
    return lax.ppermute(last, "rows", up), lax.ppermute(first, "rows", down)


def chebyshev(tiles, slots, start_vectors):
    rows = start_vectors.shape[0] // CHUNKS
    halo = HB * BS
    current = [start_vectors[c * rows:(c + 1) * rows] for c in range(CHUNKS)]
    previous = [None] * CHUNKS
    halos = [exchange_edges(x[:, x.shape[1] - halo:], x[:, :halo]) for x in current]
    band = band_matrix(tiles, slots)
    for step in range(STEPS):
        more = step < STEPS - 1
        for c in range(CHUNKS):
            following, *edges = filter_step(halos[c], current[c], band, previous[c], more)
            previous[c], current[c] = current[c], following
            if more:
                halos[c] = exchange_edges(*edges)
    return current


def lane(x, j):
    return jnp.broadcast_to(x[:, j:j + 1], x.shape)


def row(x, i):
    return jnp.broadcast_to(x[i:i + 1, :], x.shape)


def total_of(terms):
    while len(terms) > 1:
        terms = [x + y for x, y in zip(terms[::2], terms[1::2])] + terms[len(terms) & ~1:]
    return terms[0]


def small_factor(columns):
    a = {(i, j): row(columns[j], i) for j in range(SUB) for i in range(j, SUB)}
    factor, inverse = {}, {}
    for j in range(SUB):
        root = lax.rsqrt(a[j, j])
        inverse[j, j] = root
        for i in range(j + 1, SUB):
            factor[i, j] = a[i, j] * root
        for k in range(j + 1, SUB):
            for i in range(k, SUB):
                a[i, k] = a[i, k] - factor[i, j] * factor[k, j]
        for k in range(j):
            terms = [factor[j, i] * inverse[i, k] for i in range(k, j)]
            inverse[j, k] = total_of(terms) * -root
    return inverse


def inverse_factor(block):
    strips = NB // SUB
    left = [block[SUB * t:SUB * (t + 1), :] for t in range(strips)]
    rows = lax.broadcasted_iota(jnp.int32, (SUB, NB), 0)
    lanes = lax.broadcasted_iota(jnp.int32, (SUB, NB), 1)
    right = [jnp.where(lanes == rows + SUB * t, 1.0, 0.0) for t in range(strips)]
    done = []
    columns = [lane(left[0], j) for j in range(SUB)]
    for s in range(strips):
        inverse = small_factor(columns)
        factors = {}
        for t in range(s + 1, strips):
            old = [lane(left[t], SUB * s + j) for j in range(SUB)]
            factors[t] = [
                total_of([old[m] * inverse[j, m] for m in range(j + 1)]) for j in range(SUB)
            ]
            if t == s + 1:
                ahead = [lane(left[t], SUB * t + j) for j in range(SUB)]
                columns = [
                    ahead[j] - total_of([x * row(x, j) for x in factors[t]]) for j in range(SUB)
                ]
        upper_rows = [row(left[s], j) for j in range(SUB)]
        solved_rows = [row(right[s], j) for j in range(SUB)]
        spread = []
        for j in range(SUB):
            column = jnp.where(rows == j, inverse[j, j], 0.0)
            for i in range(j + 1, SUB):
                column = jnp.where(rows == i, inverse[i, j], column)
            spread.append(column)
        upper = total_of([x * y for x, y in zip(spread, upper_rows)])
        solved = total_of([x * y for x, y in zip(spread, solved_rows)])
        done.append(solved)
        upper_rows = [row(upper, j) for j in range(SUB)]
        solved_rows = [row(solved, j) for j in range(SUB)]
        for t in range(s + 1, strips):
            left[t] = left[t] - total_of([x * y for x, y in zip(factors[t], upper_rows)])
            right[t] = right[t] - total_of([x * y for x, y in zip(factors[t], solved_rows)])
    return jnp.concatenate(done, axis=0)


def eliminate(gram_ref, field_ref, low, done, total_ref, steps):
    for ref in (*low, *done):
        ref[...] = jnp.zeros_like(ref)

    def step(k, carry):
        here = pl.ds(pl.multiple_of(k * NB, NB), NB)
        mine = (low[0][here, :], low[1][here, :])
        block = gram_ref[here, here] - dot3(mine, mine, NT)
        inverse = split(inverse_factor(block))
        column = gram_ref[:, here] - dot3((low[0][...], low[1][...]), mine, NT)
        field = field_ref[here, :] - dot3(mine, (done[0][...], done[1][...]), NN)
        low[0][:, here], low[1][:, here] = split(dot3(split(column), inverse, NT))
        solved = dot3(inverse, split(field), NN)
        total_ref[here, :] = solved
        done[0][here, :], done[1][here, :] = split(solved)
        return carry

    lax.fori_loop(0, steps, step, 0)


def elimination_scratch(size, columns):
    shapes = ((size, size), (size, columns))
    return [pltpu.VMEM(shape, jnp.bfloat16) for shape in shapes for part in range(2)]


def factor_kernel(scale, place_ref, gram_ref, field_ref, out_ref, low0, low1, done0, done1, total):
    width = out_ref.shape[0]
    place = place_ref[0]
    steps = ((place + 1) * width + NB - 1) // NB
    eliminate(gram_ref, field_ref, (low0, low1), (done0, done1), total, steps)
    out_ref[...] = total[pl.ds(pl.multiple_of(place * width, SUB), width), :] * scale


def factor_and_solve(gram, field, place, width, scale):
    size, columns = field.shape
    return pl.pallas_call(
        functools.partial(factor_kernel, scale),
        out_shape=jax.ShapeDtypeStruct((width, columns), jnp.float32),
        in_specs=[SCALARS, WHOLE, WHOLE],
        out_specs=WHOLE,
        scratch_shapes=elimination_scratch(size, columns)
        + [pltpu.VMEM((size, columns), jnp.float32)],
        compiler_params=ROOMY,
        name="factor_and_solve",
    )(place, gram, field)


def joined(refs):
    return jnp.concatenate([ref[...] for ref in refs], axis=0)


def scatter_order(start, rows):
    quarter = start // (rows // 4)
    return ((quarter % 2) * 2 + quarter // 2 - quarter) * (rows // 4) + start


def own_gram_kernel(*refs):
    field, out_ref = joined(refs[:-1]), refs[-1]
    high, low = split(field)
    rows, unit = out_ref.shape[0], NB // 2
    for i in range(field.shape[0] // NB):
        here = slice(i * NB, (i + 1) * NB)
        end = (i + 1) * NB
        product = dot3((high[here], low[here]), (high[:end], low[:end]), NT)
        for j in range(i + 1):
            for part in range(0, NB, unit):
                start = scatter_order((i * (i + 1) // 2 + j) * NB + part, rows)
                out_ref[start:start + unit, :] = product[part:part + unit, j * NB:(j + 1) * NB]


def own_gram(field):
    blocks = sum(part.shape[0] for part in field) // NB
    rows = blocks * (blocks + 1) // 2 * NB
    return pl.pallas_call(
        own_gram_kernel,
        out_shape=jax.ShapeDtypeStruct((rows, NB), jnp.float32),
        in_specs=[WHOLE] * len(field),
        out_specs=WHOLE,
        compiler_params=ROOMY,
        name="own_gram",
    )(*field)


def cross_gram_kernel(*refs):
    half = (len(refs) - 1) // 2
    out_ref = refs[-1]
    mine, other = split(joined(refs[:half])), split(joined(refs[half:-1]))
    rows = out_ref.shape[0]
    blocks = mine[0].shape[0] // NB
    for i in range(blocks):
        here = slice(i * NB, (i + 1) * NB)
        product = dot3((mine[0][here], mine[1][here]), other, NT)
        for j in range(blocks):
            start = scatter_order((i * blocks + j) * NB, rows)
            out_ref[start:start + NB, :] = product[:, j * NB:(j + 1) * NB]


def cross_gram(field, other):
    size = sum(part.shape[0] for part in field)
    return pl.pallas_call(
        cross_gram_kernel,
        out_shape=jax.ShapeDtypeStruct((size * size // NB, NB), jnp.float32),
        in_specs=[WHOLE] * (2 * len(field)),
        out_specs=WHOLE,
        compiler_params=ROOMY,
        name="cross_gram",
    )(*field, *other)


def fetch(pairs, sems):
    copies = [pltpu.make_async_copy(x, y, sems.at[i]) for i, (x, y) in enumerate(pairs)]
    for copy in copies:
        copy.start()
    for copy in copies:
        copy.wait()


def rows_of(ref, start, rows):
    return ref.at[pl.ds(pl.multiple_of(start, SUB), rows), :]


def stacked(parts, target, columns):
    rows = parts[0].shape[0]
    return [(part, target.at[i * rows:(i + 1) * rows, :columns]) for i, part in enumerate(parts)]


def lower_blocks(flat, gram_ref):
    blocks = gram_ref.shape[0] // NB
    for i in range(blocks):
        for j in range(blocks):
            place = i * (i + 1) // 2 + j
            block = flat[place * NB:(place + 1) * NB, :] if j <= i else jnp.zeros((NB, NB), jnp.float32)
            gram_ref[i * NB:(i + 1) * NB, j * NB:(j + 1) * NB] = block


def first_half_kernel(where_ref, *refs):
    pieces, mine, other = refs[:4], refs[4:4 + CHUNKS], refs[4 + CHUNKS:4 + 2 * CHUNKS]
    top_ref, inverse_ref, flat, gram, field, total, low0, low1, done0, done1, sems = refs[4 + 2 * CHUNKS:]
    place, near, far = where_ref[0], where_ref[1], where_ref[2]
    size, columns = top_ref.shape
    rows = pieces[0].shape[1]
    pairs = [
        (piece.at[j], rows_of(flat, ((near ^ i) * 4 + (far ^ j)) * rows, rows))
        for i, piece in enumerate(pieces) for j in range(4)
    ]

    @pl.when(place == 0)
    def _():
        fetch(pairs + stacked(mine, field, columns), sems)

    @pl.when(place != 0)
    def _():
        fetch(pairs + stacked(other, field, columns), sems)

    lower_blocks(flat, gram)
    rows = lax.broadcasted_iota(jnp.int32, (size, size), 0)
    lanes = lax.broadcasted_iota(jnp.int32, (size, size), 1)
    field[:, columns:] = jnp.where(rows == lanes, 1.0, 0.0)
    eliminate(gram, field, (low0, low1), (done0, done1), total, size // NB)
    top_ref[...] = total[:, :columns]
    inverse_ref[...] = total[:, columns:]


def first_half(where, pieces, mine, other):
    size, columns = sum(part.shape[0] for part in mine), mine[0].shape[1]
    f32 = jnp.float32
    flat_rows = 4 * pieces[0].shape[0] * pieces[0].shape[1]
    operands = (*pieces, *mine, *other)
    shapes = ((size, columns), (size, size))
    return pl.pallas_call(
        first_half_kernel,
        out_shape=tuple(jax.ShapeDtypeStruct(shape, f32) for shape in shapes),
        in_specs=[SCALARS] + [AFAR] * len(operands),
        out_specs=(WHOLE, WHOLE),
        scratch_shapes=[
            pltpu.VMEM((flat_rows, NB), f32),
            pltpu.VMEM((size, size), f32),
            pltpu.VMEM((size, columns + size), f32),
            pltpu.VMEM((size, columns + size), f32),
        ] + elimination_scratch(size, columns + size) + [pltpu.SemaphoreType.DMA((16 + CHUNKS,))],
        compiler_params=ROOMY,
        cost_estimate=pl.CostEstimate(flops=2 * 10 ** 10, bytes_accessed=10 ** 7, transcendentals=0),
        name="first_half",
    )(where, *operands)


def second_half_kernel(scale, where_ref, *refs):
    rest, mine = refs[0], refs[1:1 + CHUNKS]
    top_ref, inverse_ref, out_ref = refs[1 + CHUNKS:4 + CHUNKS]
    flat, corner, gram, field, total, low0, low1, done0, done1, sems = refs[4 + CHUNKS:]
    place = where_ref[0]
    size, columns = top_ref.shape
    blocks = size // NB
    rows = rest.shape[2] - NB

    @pl.when(place == 0)
    def _():
        out_ref[...] = top_ref[...] * scale

    @pl.when(place != 0)
    def _():
        pairs = stacked(mine, field, columns)
        for i in range(4):
            for j in range(4):
                pairs.append((rest.at[i, j, :rows], rows_of(flat, (i * 4 + j) * rows, rows)))
                pairs.append((rest.at[i, j, rows:], corner.at[i * NB:(i + 1) * NB, j * NB:(j + 1) * NB]))
        fetch(pairs, sems)
        lower_blocks(flat, gram)
        low = split(dot3(split(corner[...]), split(inverse_ref[...]), NT))
        gram[...] = gram[...] - dot3(low, low, NT)
        field[...] = field[...] - dot3(low, split(top_ref[...]), NN)
        eliminate(gram, field, (low0, low1), (done0, done1), total, blocks)
        out_ref[...] = total[...] * scale


def second_half(where, rest, mine, top, inverse, scale):
    size, columns = top.shape
    f32 = jnp.float32
    return pl.pallas_call(
        functools.partial(second_half_kernel, scale),
        out_shape=jax.ShapeDtypeStruct((size, columns), f32),
        in_specs=[SCALARS] + [AFAR] * (1 + CHUNKS) + [WHOLE] * 2,
        out_specs=WHOLE,
        scratch_shapes=[
            pltpu.VMEM((16 * (rest.shape[2] - NB), NB), f32),
            pltpu.VMEM((size, size), f32),
            pltpu.VMEM((size, size), f32),
            pltpu.VMEM((size, columns), f32),
            pltpu.VMEM((size, columns), f32),
        ] + elimination_scratch(size, columns) + [pltpu.SemaphoreType.DMA((32 + CHUNKS,))],
        compiler_params=ROOMY,
        name="second_half",
    )(where, rest, *mine, top, inverse)


NEAR, FAR = 1, 4


def send(x, stride, planes=None):
    devices, sides = lax.axis_size("rows"), lax.axis_size("vecs")
    pairs = [
        (i * sides + v, (i ^ stride) * sides + v)
        for i in range(devices) for v in (range(sides) if planes is None else planes)
    ]
    return lax.ppermute(x, ("rows", "vecs"), pairs)


def send_up(x, stride):
    devices, sides = lax.axis_size("rows"), lax.axis_size("vecs")
    pairs = [(i * sides, (i ^ stride) * sides + 1) for i in range(devices)]
    return lax.ppermute(x, ("rows", "vecs"), pairs)


def swap_half(x, bit, stride, planes=None):
    halves = x.reshape(2, -1, NB)
    kept = lax.dynamic_index_in_dim(halves, bit, 0, keepdims=False)
    given = lax.dynamic_index_in_dim(halves, 1 - bit, 0, keepdims=False)
    return kept + send(given, stride, planes)


def reduce_group(x, here, stride, planes=None):
    parts = x.reshape(4, -1, NB)
    total = lax.dynamic_index_in_dim(parts, here, 0, keepdims=False)
    others = [
        send(lax.dynamic_index_in_dim(parts, here ^ i, 0, keepdims=False), i * stride, planes)
        for i in range(1, 4)
    ]
    return total + others[0] + (others[1] + others[2])


def orthonormalize_planes(current, scale):
    together = lax.optimization_barrier
    rank = lax.axis_index("rows")
    place = lax.axis_index("vecs")
    near, far = rank % 4, rank // 4
    where = jnp.stack([place, near, far]).astype(jnp.int32)
    near_groups = [list(range(4 * g, 4 * g + 4)) for g in range(4)]
    far_groups = [list(range(g, 16, 4)) for g in range(4)]
    below = [send_up(part, 0) for part in current]
    own, below[0] = together((current, below[0]))
    half = swap_half(own_gram(own), near % 2, 1)
    fourth = swap_half(half, near // 2, 2)
    fourth, *below = together((fourth, *below))
    corner = cross_gram(current, below)
    corner = swap_half(corner, near % 2, 1, (1,))
    mine = reduce_group(fourth, far, FAR)
    mine, corner = together((mine, corner))
    first = jnp.where(place == 0, mine, send_up(mine, 0))
    corner = swap_half(corner, near // 2, 2, (1,))
    first, corner = together((first, corner))
    first = jnp.stack([first] + [send(first, i * FAR) for i in range(1, 4)])
    corner = reduce_group(corner, far, FAR, (1,))
    first, corner = together((first, corner))
    rest = jnp.concatenate([mine, corner], axis=0)
    rest = lax.all_gather(rest, "rows", axis_index_groups=far_groups)
    pieces = [first] + [send(first, i * NEAR) for i in range(1, 4)]
    pieces, rest = together((pieces, rest))
    rest = lax.all_gather(rest, "rows", axis_index_groups=near_groups)
    top, inverse = first_half(where, pieces, current, below)
    return second_half(where, rest, current, top, inverse, scale)


def orthonormalize(current, scale):
    current = jnp.concatenate(current, axis=0)
    width = current.shape[0]
    gathered = lax.all_gather(current, "vecs", axis=0, tiled=True)
    partial_rows = jnp.einsum("mn,kn->mk", current, gathered, precision=lax.Precision.HIGHEST)
    summed_rows = lax.psum(partial_rows, "rows")
    gram = lax.all_gather(summed_rows, "vecs", axis=0, tiled=True)
    place = lax.axis_index("vecs").astype(jnp.int32)[None]
    return factor_and_solve(gram, gathered, place, width, scale)


def body(tiles, columns, start_vectors):
    blocks_here = tiles.shape[0]
    total_blocks = blocks_here * lax.axis_size("rows")
    first_block = lax.axis_index("rows") * blocks_here
    global_rows = first_block + jnp.arange(blocks_here, dtype=jnp.int32)
    offsets = jnp.mod(columns - global_rows[:, None] + HB, total_blocks)
    slots = jnp.arange(blocks_here, dtype=jnp.int32)[:, None] + offsets
    current = chebyshev(tiles, slots, start_vectors)
    scale = float((total_blocks * BS) ** 0.5)
    fits = (
        lax.axis_size("vecs") == 2
        and lax.axis_size("rows") == 16
        and start_vectors.shape[0] == 4 * NB
    )
    return (orthonormalize_planes if fits else orthonormalize)(current, scale)


def solution(mesh):
    placed = (P("rows", None, None, None), P("rows", None), P("vecs", "rows"))
    return jax.shard_map(
        body, mesh=mesh, in_specs=placed, out_specs=P("vecs", "rows"), check_vma=False
    )
```

```python
import functools

import jax
import jax.numpy as jnp
from jax import lax
from jax.experimental import pallas as pl
from jax.experimental.pallas import tpu as pltpu
from jax.sharding import PartitionSpec as P

BS = 128
HB = 3
STEPS = 4
NB = 128
SUB = 8
CHUNKS = 2
NT = (((1,), (1,)), ((), ()))
NN = (((1,), (0,)), ((), ()))
SCALARS = pl.BlockSpec(memory_space=pltpu.SMEM)
WHOLE = pl.BlockSpec(memory_space=pltpu.VMEM)
AFAR = pl.BlockSpec(memory_space=pl.ANY)
ROOMY = pltpu.CompilerParams(vmem_limit_bytes=28 * 2 ** 20)
ALONE = pltpu.CompilerParams(vmem_limit_bytes=48 * 2 ** 20)


def split(x):
    high = x.astype(jnp.bfloat16)
    return high, (x - high.astype(jnp.float32)).astype(jnp.bfloat16)


def dot3(a, b, dims):
    def dot(x, y):
        return lax.dot_general(x, y, dims, preferred_element_type=jnp.float32)

    return dot(a[0], b[0]) + (dot(a[0], b[1]) + dot(a[1], b[0]))


def band_kernel(slots_ref, tiles_ref, band_ref):
    band_ref[...] = jnp.zeros_like(band_ref)
    for b in range(tiles_ref.shape[0]):
        for t in range(tiles_ref.shape[1]):
            start = pl.multiple_of(slots_ref[b, t] * BS, BS)
            flipped = tiles_ref[b, t].astype(jnp.float32).T
            band_ref[pl.ds(start, BS), b * BS:(b + 1) * BS] = flipped.astype(jnp.bfloat16)


def band_matrix(tiles, slots):
    blocks = tiles.shape[0]
    return pl.pallas_call(
        band_kernel,
        out_shape=jax.ShapeDtypeStruct(((blocks + 2 * HB) * BS, blocks * BS), jnp.bfloat16),
        in_specs=[SCALARS, WHOLE],
        out_specs=WHOLE,
        compiler_params=ROOMY,
        name="band_matrix",
    )(slots, tiles)


def step_kernel(has_previous, has_edges, *refs):
    before_ref, current_ref, after_ref, band_ref = refs[:4]
    outs = refs[4 + has_previous:]
    parts = [ref[...] for ref in (before_ref, current_ref, after_ref)]
    highs, lows = zip(*[split(part) for part in parts])
    high, low = jnp.concatenate(highs, axis=1), jnp.concatenate(lows, axis=1)
    columns = current_ref.shape[1]
    blocks = columns // BS
    halo = HB * BS
    for b in range(0, blocks, 2):
        end = min(b + 2, blocks)
        here = slice(b * BS, end * BS)
        depth = slice(b * BS, (end + 2 * HB) * BS)
        band = band_ref[depth, here]

        def dot(x):
            return jnp.dot(x[:, depth], band, preferred_element_type=jnp.float32)

        result = dot(high) + dot(low)
        if has_previous:
            result = 2.0 * result - refs[4][:, here]
        outs[0][:, here] = result
    if has_edges:
        outs[1][...] = outs[0][:, columns - halo:]
        outs[2][...] = outs[0][:, :halo]


def filter_step(halos, current, band, previous, has_edges):
    before, after = halos
    width, columns = current.shape
    f32 = jnp.float32
    edge = jax.ShapeDtypeStruct((width, HB * BS), f32)
    shapes = (jax.ShapeDtypeStruct((width, columns), f32),) + (edge, edge) * has_edges
    operands = (before, current, after, band) + ((previous,) if previous is not None else ())
    return pl.pallas_call(
        functools.partial(step_kernel, previous is not None, has_edges),
        out_shape=shapes,
        in_specs=[WHOLE] * len(operands),
        out_specs=(WHOLE,) * len(shapes),
        compiler_params=ROOMY,
        cost_estimate=pl.CostEstimate(
            flops=4 * width * columns * (2 + 2 * HB) * BS,
            bytes_accessed=4 * width * columns * 6,
            transcendentals=0,
        ),
        name="filter_step",
    )(*operands)


def exchange_edges(last, first):
    devices = lax.axis_size("rows")
    up = [(i, (i + 1) % devices) for i in range(devices)]
    down = [(j, i) for i, j in up]
    return lax.ppermute(last, "rows", up), lax.ppermute(first, "rows", down)


def chebyshev(tiles, slots, start_vectors):
    rows = start_vectors.shape[0] // CHUNKS
    halo = HB * BS
    current = [start_vectors[c * rows:(c + 1) * rows] for c in range(CHUNKS)]
    previous = [None] * CHUNKS
    halos = [exchange_edges(x[:, x.shape[1] - halo:], x[:, :halo]) for x in current]
    band = band_matrix(tiles, slots)
    for step in range(STEPS):
        more = step < STEPS - 1
        for c in range(CHUNKS):
            halos[c], current[c - 1] = lax.optimization_barrier((halos[c], current[c - 1]))
            following, *edges = filter_step(halos[c], current[c], band, previous[c], more)
            previous[c], current[c] = current[c], following
            if more:
                halos[c] = exchange_edges(*edges)
    return current


def lane(x, j):
    return jnp.broadcast_to(x[:, j:j + 1], x.shape)


def row(x, i):
    return jnp.broadcast_to(x[i:i + 1, :], x.shape)


def total_of(terms):
    while len(terms) > 1:
        terms = [x + y for x, y in zip(terms[::2], terms[1::2])] + terms[len(terms) & ~1:]
    return terms[0]


def small_factor(columns):
    a = {(i, j): row(columns[j], i) for j in range(SUB) for i in range(j, SUB)}
    factor, inverse = {}, {}
    for j in range(SUB):
        root = lax.rsqrt(a[j, j])
        inverse[j, j] = root
        for i in range(j + 1, SUB):
            factor[i, j] = a[i, j] * root
        for k in range(j + 1, SUB):
            for i in range(k, SUB):
                a[i, k] = a[i, k] - factor[i, j] * factor[k, j]
        for k in range(j):
            terms = [factor[j, i] * inverse[i, k] for i in range(k, j)]
            inverse[j, k] = total_of(terms) * -root
    return inverse


def inverse_factor(block):
    strips = NB // SUB
    left = [block[SUB * t:SUB * (t + 1), :] for t in range(strips)]
    rows = lax.broadcasted_iota(jnp.int32, (SUB, NB), 0)
    lanes = lax.broadcasted_iota(jnp.int32, (SUB, NB), 1)
    right = [jnp.where(lanes == rows + SUB * t, 1.0, 0.0) for t in range(strips)]
    done = []
    columns = [lane(left[0], j) for j in range(SUB)]
    for s in range(strips):
        inverse = small_factor(columns)
        factors = {}
        for t in range(s + 1, strips):
            old = [lane(left[t], SUB * s + j) for j in range(SUB)]
            factors[t] = [
                total_of([old[m] * inverse[j, m] for m in range(j + 1)]) for j in range(SUB)
            ]
            if t == s + 1:
                ahead = [lane(left[t], SUB * t + j) for j in range(SUB)]
                columns = [
                    ahead[j] - total_of([x * row(x, j) for x in factors[t]]) for j in range(SUB)
                ]
        upper_rows = [row(left[s], j) for j in range(SUB)]
        solved_rows = [row(right[s], j) for j in range(SUB)]
        spread = []
        for j in range(SUB):
            column = jnp.where(rows == j, inverse[j, j], 0.0)
            for i in range(j + 1, SUB):
                column = jnp.where(rows == i, inverse[i, j], column)
            spread.append(column)
        upper = total_of([x * y for x, y in zip(spread, upper_rows)])
        solved = total_of([x * y for x, y in zip(spread, solved_rows)])
        done.append(solved)
        upper_rows = [row(upper, j) for j in range(SUB)]
        solved_rows = [row(solved, j) for j in range(SUB)]
        for t in range(s + 1, strips):
            left[t] = left[t] - total_of([x * y for x, y in zip(factors[t], upper_rows)])
            right[t] = right[t] - total_of([x * y for x, y in zip(factors[t], solved_rows)])
    return jnp.concatenate(done, axis=0)


def eliminate(gram_ref, field_ref, low, done, total_ref, steps):
    for ref in (*low, *done):
        ref[...] = jnp.zeros_like(ref)

    def step(k, carry):
        here = pl.ds(pl.multiple_of(k * NB, NB), NB)
        mine = (low[0][here, :], low[1][here, :])
        block = gram_ref[here, here] - dot3(mine, mine, NT)
        inverse = split(inverse_factor(block))
        column = gram_ref[:, here] - dot3((low[0][...], low[1][...]), mine, NT)
        field = field_ref[here, :] - dot3(mine, (done[0][...], done[1][...]), NN)
        low[0][:, here], low[1][:, here] = split(dot3(split(column), inverse, NT))
        solved = dot3(inverse, split(field), NN)
        total_ref[here, :] = solved
        done[0][here, :], done[1][here, :] = split(solved)
        return carry

    lax.fori_loop(0, steps, step, 0)


def elimination_scratch(size, columns):
    shapes = ((size, size), (size, columns))
    return [pltpu.VMEM(shape, jnp.bfloat16) for shape in shapes for part in range(2)]


def factor_kernel(scale, place_ref, gram_ref, field_ref, out_ref, low0, low1, done0, done1, total):
    width = out_ref.shape[0]
    place = place_ref[0]
    steps = ((place + 1) * width + NB - 1) // NB
    eliminate(gram_ref, field_ref, (low0, low1), (done0, done1), total, steps)
    out_ref[...] = total[pl.ds(pl.multiple_of(place * width, SUB), width), :] * scale


def factor_and_solve(gram, field, place, width, scale):
    size, columns = field.shape
    return pl.pallas_call(
        functools.partial(factor_kernel, scale),
        out_shape=jax.ShapeDtypeStruct((width, columns), jnp.float32),
        in_specs=[SCALARS, WHOLE, WHOLE],
        out_specs=WHOLE,
        scratch_shapes=elimination_scratch(size, columns)
        + [pltpu.VMEM((size, columns), jnp.float32)],
        compiler_params=ROOMY,
        name="factor_and_solve",
    )(place, gram, field)


def joined(refs):
    return jnp.concatenate([ref[...] for ref in refs], axis=0)


def scatter_order(start, rows):
    quarter = start // (rows // 4)
    return ((quarter % 2) * 2 + quarter // 2 - quarter) * (rows // 4) + start


def own_gram_kernel(*refs):
    field, out_ref = joined(refs[:-1]), refs[-1]
    high, low = split(field)
    rows, unit = out_ref.shape[0], NB // 2
    for i in range(field.shape[0] // NB):
        here = slice(i * NB, (i + 1) * NB)
        end = (i + 1) * NB
        product = dot3((high[here], low[here]), (high[:end], low[:end]), NT)
        for j in range(i + 1):
            for part in range(0, NB, unit):
                start = scatter_order((i * (i + 1) // 2 + j) * NB + part, rows)
                out_ref[start:start + unit, :] = product[part:part + unit, j * NB:(j + 1) * NB]


def own_gram(field):
    blocks = sum(part.shape[0] for part in field) // NB
    rows = blocks * (blocks + 1) // 2 * NB
    return pl.pallas_call(
        own_gram_kernel,
        out_shape=jax.ShapeDtypeStruct((rows, NB), jnp.float32),
        in_specs=[WHOLE] * len(field),
        out_specs=WHOLE,
        compiler_params=ROOMY,
        name="own_gram",
    )(*field)


def cross_gram_kernel(*refs):
    half = (len(refs) - 1) // 2
    out_ref = refs[-1]
    mine, other = split(joined(refs[:half])), split(joined(refs[half:-1]))
    rows = out_ref.shape[0]
    blocks = mine[0].shape[0] // NB
    for i in range(blocks):
        here = slice(i * NB, (i + 1) * NB)
        product = dot3((mine[0][here], mine[1][here]), other, NT)
        for j in range(blocks):
            start = scatter_order((i * blocks + j) * NB, rows)
            out_ref[start:start + NB, :] = product[:, j * NB:(j + 1) * NB]


def cross_gram(field, other):
    size = sum(part.shape[0] for part in field)
    return pl.pallas_call(
        cross_gram_kernel,
        out_shape=jax.ShapeDtypeStruct((size * size // NB, NB), jnp.float32),
        in_specs=[WHOLE] * (2 * len(field)),
        out_specs=WHOLE,
        compiler_params=ROOMY,
        name="cross_gram",
    )(*field, *other)


def fetch(pairs, sems):
    copies = [pltpu.make_async_copy(x, y, sems.at[i]) for i, (x, y) in enumerate(pairs)]
    for copy in copies:
        copy.start()
    for copy in copies:
        copy.wait()


def rows_of(ref, start, rows):
    return ref.at[pl.ds(pl.multiple_of(start, SUB), rows), :]


def stacked(parts, target, columns):
    rows = parts[0].shape[0]
    return [(part, target.at[i * rows:(i + 1) * rows, :columns]) for i, part in enumerate(parts)]


def lower_blocks(flat, gram_ref, first):
    blocks = gram_ref.shape[0] // NB
    for i in range(blocks):
        for j in range(blocks):
            place = (first + i) * (first + i + 1) // 2 + first + j
            block = flat[place * NB:(place + 1) * NB, :] if j <= i else jnp.zeros((NB, NB), jnp.float32)
            gram_ref[i * NB:(i + 1) * NB, j * NB:(j + 1) * NB] = block


def inverted(low, first, second):
    return -dot3(split(second), split(dot3(low, first, NN)), NN)


def identity(size):
    rows = lax.broadcasted_iota(jnp.int32, (size, size), 0)
    lanes = lax.broadcasted_iota(jnp.int32, (size, size), 1)
    return jnp.where(rows == lanes, 1.0, 0.0)


def first_quarter_kernel(where_ref, *refs):
    pieces, mine, other, top_ref, inverse_ref = refs[:4], refs[4], refs[5], refs[6], refs[7]
    flat, gram, field, total, low0, low1, done0, done1, sems = refs[8:]
    place, near, far = where_ref[0], where_ref[1], where_ref[2]
    size, columns = top_ref.shape
    rows = pieces[0].shape[1]
    pairs = [
        (piece.at[j], rows_of(flat, ((near ^ i) * 4 + (far ^ j)) * rows, rows))
        for i, piece in enumerate(pieces) for j in range(4)
    ]

    @pl.when(place == 0)
    def _():
        fetch(pairs + stacked([mine], field, columns), sems)

    @pl.when(place != 0)
    def _():
        fetch(pairs + stacked([other], field, columns), sems)

    lower_blocks(flat, gram, 0)
    field[:, columns:] = identity(size)
    eliminate(gram, field, (low0, low1), (done0, done1), total, size // NB)
    fetch([(total.at[:, :columns], top_ref), (total.at[:, columns:], inverse_ref)], sems)


def second_quarter_kernel(where_ref, *refs):
    pieces, mine, other, top_in, inverse_in, top_ref, inverse_ref = refs[:4], *refs[4:10]
    flat, gram, corner, top, inverse, field, total, low0, low1, done0, done1, sems = refs[10:]
    place, near, far = where_ref[0], where_ref[1], where_ref[2]
    size, columns = mine.shape
    rows = pieces[0].shape[1]
    pairs = [
        (piece.at[j], rows_of(flat, ((near ^ i) * 4 + (far ^ j)) * rows, rows))
        for i, piece in enumerate(pieces) for j in range(4)
    ] + [(top_in, top), (inverse_in, inverse)]

    @pl.when(place == 0)
    def _():
        fetch(pairs + stacked([mine], field, columns), sems)

    @pl.when(place != 0)
    def _():
        fetch(pairs + stacked([other], field, columns), sems)

    blocks = size // NB
    lower_blocks(flat, gram, blocks)
    for i in range(blocks):
        for j in range(blocks):
            start = ((blocks + i) * (blocks + i + 1) // 2 + j) * NB
            corner[i * NB:(i + 1) * NB, j * NB:(j + 1) * NB] = flat[start:start + NB, :]
    first = split(inverse[...])
    low = split(dot3(split(corner[...]), first, NT))
    gram[...] = gram[...] - dot3(low, low, NT)
    field[:, :columns] = field[:, :columns] - dot3(low, split(top[...]), NN)
    field[:, columns:] = identity(size)
    eliminate(gram, field, (low0, low1), (done0, done1), total, blocks)
    corner[...] = inverted(low, first, total[:, columns:])
    gram[...] = jnp.zeros_like(gram)
    fetch([
        (top, top_ref.at[:size]),
        (total.at[:, :columns], top_ref.at[size:]),
        (inverse, inverse_ref.at[:size, :size]),
        (gram, inverse_ref.at[:size, size:]),
        (corner, inverse_ref.at[size:, :size]),
        (total.at[:, columns:], inverse_ref.at[size:, size:]),
    ], sems)


def quarter(kernel, where, pieces, mine, other, *before):
    size, columns = mine.shape
    f32 = jnp.float32
    flat_rows = 4 * pieces[0].shape[0] * pieces[0].shape[1]
    operands = (*pieces, mine, other, *before)
    results = 2 * size if before else size
    square, wide = pltpu.VMEM((size, size), f32), pltpu.VMEM((size, columns + size), f32)
    earlier = [square, pltpu.VMEM((size, columns), f32), square] if before else []
    return pl.pallas_call(
        kernel,
        out_shape=tuple(jax.ShapeDtypeStruct((results, n), f32) for n in (columns, results)),
        in_specs=[SCALARS] + [AFAR] * len(operands),
        out_specs=(AFAR, AFAR),
        scratch_shapes=[pltpu.VMEM((flat_rows, NB), f32), square] + earlier + [wide, wide]
        + elimination_scratch(size, columns + size) + [pltpu.SemaphoreType.DMA((19,))],
        compiler_params=ALONE,
        cost_estimate=pl.CostEstimate(flops=10 ** 10, bytes_accessed=10 ** 7, transcendentals=0),
        name="second_quarter" if before else "first_quarter",
    )(where, *operands)


def second_half_kernel(scale, where_ref, *refs):
    pieces, corners, mine = refs[0], refs[1:5], refs[5:5 + CHUNKS]
    top_in, inverse_in, out_ref = refs[5 + CHUNKS:8 + CHUNKS]
    flat, corner, gram, top, inverse, field, total, low0, low1, done0, done1, sems = refs[8 + CHUNKS:]
    place, near, far = where_ref[0], where_ref[1], where_ref[2]
    size, columns = top.shape
    blocks = size // NB
    rows = pieces.shape[2]

    @pl.when(place == 0)
    def _():
        fetch([(top_in, top)], sems)
        out_ref[...] = top[...] * scale

    @pl.when(place != 0)
    def _():
        pairs = stacked(mine, field, columns) + [(top_in, top), (inverse_in, inverse)]
        for i in range(4):
            for j in range(4):
                pairs.append((pieces.at[i, j], rows_of(flat, (i * 4 + (far ^ j)) * rows, rows)))
                lanes = pl.ds(pl.multiple_of((far ^ j) * NB, NB), NB)
                target = corner.at[pl.ds(pl.multiple_of((near ^ i) * NB, NB), NB), lanes]
                pairs.append((corners[i].at[j], target))
        fetch(pairs, sems)
        lower_blocks(flat, gram, 0)
        low = split(dot3(split(corner[...]), split(inverse[...]), NT))
        gram[...] = gram[...] - dot3(low, low, NT)
        field[...] = field[...] - dot3(low, split(top[...]), NN)
        eliminate(gram, field, (low0, low1), (done0, done1), total, blocks)
        out_ref[...] = total[...] * scale


def second_half(where, pieces, corners, mine, top, inverse, scale):
    size, columns = top.shape
    f32 = jnp.float32
    square, wide = pltpu.VMEM((size, size), f32), pltpu.VMEM((size, columns), f32)
    return pl.pallas_call(
        functools.partial(second_half_kernel, scale),
        out_shape=jax.ShapeDtypeStruct((size, columns), f32),
        in_specs=[SCALARS] + [AFAR] * (7 + CHUNKS),
        out_specs=WHOLE,
        scratch_shapes=[
            pltpu.VMEM((16 * pieces.shape[2], NB), f32), square, square, wide, square, wide, wide,
        ] + elimination_scratch(size, columns) + [pltpu.SemaphoreType.DMA((34 + CHUNKS,))],
        compiler_params=ALONE,
        name="second_half",
    )(where, pieces, *corners, *mine, top, inverse)


NEAR, FAR = 1, 4


def send(x, stride, planes=None):
    devices, sides = lax.axis_size("rows"), lax.axis_size("vecs")
    pairs = [
        (i * sides + v, (i ^ stride) * sides + v)
        for i in range(devices) for v in (range(sides) if planes is None else planes)
    ]
    return lax.ppermute(x, ("rows", "vecs"), pairs)


def send_up(x, stride):
    devices, sides = lax.axis_size("rows"), lax.axis_size("vecs")
    pairs = [(i * sides, (i ^ stride) * sides + 1) for i in range(devices)]
    return lax.ppermute(x, ("rows", "vecs"), pairs)


def swap_half(x, bit, stride, planes=None):
    halves = x.reshape(2, -1, NB)
    kept = lax.dynamic_index_in_dim(halves, bit, 0, keepdims=False)
    given = lax.dynamic_index_in_dim(halves, 1 - bit, 0, keepdims=False)
    return kept + send(given, stride, planes)


def reduce_group(x, here, stride, planes=None):
    parts = x.reshape(4, -1, NB)
    total = lax.dynamic_index_in_dim(parts, here, 0, keepdims=False)
    others = [
        send(lax.dynamic_index_in_dim(parts, here ^ i, 0, keepdims=False), i * stride, planes)
        for i in range(1, 4)
    ]
    return total + others[0] + (others[1] + others[2])


def orthonormalize_planes(current, scale):
    together = lax.optimization_barrier
    rank = lax.axis_index("rows")
    place = lax.axis_index("vecs")
    near, far = rank % 4, rank // 4
    where = jnp.stack([place, near, far]).astype(jnp.int32)
    near_groups = [list(range(4 * g, 4 * g + 4)) for g in range(4)]
    below = [send_up(part, 0) for part in current]
    own, below[0] = together((current, below[0]))
    half = swap_half(own_gram(own), near % 2, 1)
    fourth = swap_half(half, near // 2, 2)
    mine = reduce_group(fourth, far, FAR)
    mine, *below = together((mine, *below))
    first = jnp.where(place == 0, mine, send_up(mine, 0))
    corner = swap_half(cross_gram(current, below), near % 2, 1, (1,))
    first, corner = together((first, corner))
    both = jnp.concatenate([first, mine], axis=0)
    both = jnp.stack([both] + [send(both, i * FAR) for i in range(1, 4)])
    corner = swap_half(corner, near // 2, 2, (1,))
    both, corner = together((both, corner))
    rows = mine.shape[0]
    first, second = both[:, :rows], both[:, rows:]
    second = lax.all_gather(second, "rows", axis_index_groups=near_groups)
    pieces = [first] + [send(first, i * NEAR) for i in range(1, 4)]
    corner = reduce_group(corner, far, FAR, (1,))
    pieces, corner = together((pieces, corner))
    top, inverse = quarter(first_quarter_kernel, where, pieces, current[0], below[0])
    corner = jnp.stack([corner] + [send(corner, i * FAR, (1,)) for i in range(1, 4)])
    top, inverse, corner = together((top, inverse, corner))
    top, inverse = quarter(second_quarter_kernel, where, pieces, current[1], below[1], top, inverse)
    corners = [corner] + [send(corner, i * NEAR, (1,)) for i in range(1, 4)]
    return second_half(where, second, corners, current, top, inverse, scale)


def orthonormalize(current, scale):
    current = jnp.concatenate(current, axis=0)
    width = current.shape[0]
    gathered = lax.all_gather(current, "vecs", axis=0, tiled=True)
    partial_rows = jnp.einsum("mn,kn->mk", current, gathered, precision=lax.Precision.HIGHEST)
    summed_rows = lax.psum(partial_rows, "rows")
    gram = lax.all_gather(summed_rows, "vecs", axis=0, tiled=True)
    place = lax.axis_index("vecs").astype(jnp.int32)[None]
    return factor_and_solve(gram, gathered, place, width, scale)


def body(tiles, columns, start_vectors):
    blocks_here = tiles.shape[0]
    total_blocks = blocks_here * lax.axis_size("rows")
    first_block = lax.axis_index("rows") * blocks_here
    global_rows = first_block + jnp.arange(blocks_here, dtype=jnp.int32)
    offsets = jnp.mod(columns - global_rows[:, None] + HB, total_blocks)
    slots = jnp.arange(blocks_here, dtype=jnp.int32)[:, None] + offsets
    current = chebyshev(tiles, slots, start_vectors)
    scale = float((total_blocks * BS) ** 0.5)
    fits = (
        lax.axis_size("vecs") == 2
        and lax.axis_size("rows") == 16
        and start_vectors.shape[0] == 4 * NB
    )
    return (orthonormalize_planes if fits else orthonormalize)(current, scale)


def solution(mesh):
    placed = (P("rows", None, None, None), P("rows", None), P("vecs", "rows"))
    return jax.shard_map(
        body, mesh=mesh, in_specs=placed, out_specs=P("vecs", "rows"), check_vma=False
    )
```

```python
import functools

import jax
import jax.numpy as jnp
from jax import lax
from jax.experimental import pallas as pl
from jax.experimental.pallas import tpu as pltpu
from jax.sharding import PartitionSpec as P

BS = 128
HB = 3
STEPS = 4
NB = 128
SUB = 8
CHUNKS = 2
NT = (((1,), (1,)), ((), ()))
NN = (((1,), (0,)), ((), ()))
SCALARS = pl.BlockSpec(memory_space=pltpu.SMEM)
WHOLE = pl.BlockSpec(memory_space=pltpu.VMEM)
AFAR = pl.BlockSpec(memory_space=pl.ANY)
ROOMY = pltpu.CompilerParams(vmem_limit_bytes=28 * 2 ** 20)
ALONE = pltpu.CompilerParams(vmem_limit_bytes=48 * 2 ** 20)


def split(x):
    high = x.astype(jnp.bfloat16)
    return high, (x - high.astype(jnp.float32)).astype(jnp.bfloat16)


def dot3(a, b, dims):
    def dot(x, y):
        return lax.dot_general(x, y, dims, preferred_element_type=jnp.float32)

    return dot(a[0], b[0]) + (dot(a[0], b[1]) + dot(a[1], b[0]))


def band_kernel(slots_ref, tiles_ref, band_ref):
    band_ref[...] = jnp.zeros_like(band_ref)
    for b in range(tiles_ref.shape[0]):
        for t in range(tiles_ref.shape[1]):
            start = pl.multiple_of(slots_ref[b, t] * BS, BS)
            flipped = tiles_ref[b, t].astype(jnp.float32).T
            band_ref[pl.ds(start, BS), b * BS:(b + 1) * BS] = flipped.astype(jnp.bfloat16)


def band_matrix(tiles, slots):
    blocks = tiles.shape[0]
    return pl.pallas_call(
        band_kernel,
        out_shape=jax.ShapeDtypeStruct(((blocks + 2 * HB) * BS, blocks * BS), jnp.bfloat16),
        in_specs=[SCALARS, WHOLE],
        out_specs=WHOLE,
        compiler_params=ROOMY,
        name="band_matrix",
    )(slots, tiles)


def step_kernel(has_previous, has_edges, *refs):
    before_ref, current_ref, after_ref, band_ref = refs[:4]
    outs = refs[4 + has_previous:]
    parts = [ref[...] for ref in (before_ref, current_ref, after_ref)]
    highs, lows = zip(*[split(part) for part in parts])
    high, low = jnp.concatenate(highs, axis=1), jnp.concatenate(lows, axis=1)
    columns = current_ref.shape[1]
    blocks = columns // BS
    halo = HB * BS
    for b in range(0, blocks, 2):
        end = min(b + 2, blocks)
        here = slice(b * BS, end * BS)
        depth = slice(b * BS, (end + 2 * HB) * BS)
        band = band_ref[depth, here]

        def dot(x):
            return jnp.dot(x[:, depth], band, preferred_element_type=jnp.float32)

        result = dot(high) + dot(low)
        if has_previous:
            result = 2.0 * result - refs[4][:, here]
        outs[0][:, here] = result
    if has_edges:
        outs[1][...] = outs[0][:, columns - halo:]
        outs[2][...] = outs[0][:, :halo]


def filter_step(halos, current, band, previous, has_edges):
    before, after = halos
    width, columns = current.shape
    f32 = jnp.float32
    edge = jax.ShapeDtypeStruct((width, HB * BS), f32)
    shapes = (jax.ShapeDtypeStruct((width, columns), f32),) + (edge, edge) * has_edges
    operands = (before, current, after, band) + ((previous,) if previous is not None else ())
    return pl.pallas_call(
        functools.partial(step_kernel, previous is not None, has_edges),
        out_shape=shapes,
        in_specs=[WHOLE] * len(operands),
        out_specs=(WHOLE,) * len(shapes),
        compiler_params=ROOMY,
        cost_estimate=pl.CostEstimate(
            flops=4 * width * columns * (2 + 2 * HB) * BS,
            bytes_accessed=4 * width * columns * 6,
            transcendentals=0,
        ),
        name="filter_step",
    )(*operands)


def exchange_edges(last, first):
    devices = lax.axis_size("rows")
    up = [(i, (i + 1) % devices) for i in range(devices)]
    down = [(j, i) for i, j in up]
    return lax.ppermute(last, "rows", up), lax.ppermute(first, "rows", down)


def chebyshev(tiles, slots, start_vectors):
    rows = start_vectors.shape[0] // CHUNKS
    halo = HB * BS
    current = [start_vectors[c * rows:(c + 1) * rows] for c in range(CHUNKS)]
    previous = [None] * CHUNKS
    halos = [exchange_edges(x[:, x.shape[1] - halo:], x[:, :halo]) for x in current]
    band = band_matrix(tiles, slots)
    for step in range(STEPS):
        more = step < STEPS - 1
        for c in range(CHUNKS):
            halos[c], current[c - 1] = lax.optimization_barrier((halos[c], current[c - 1]))
            following, *edges = filter_step(halos[c], current[c], band, previous[c], more)
            previous[c], current[c] = current[c], following
            if more:
                halos[c] = exchange_edges(*edges)
    return current


def lane(x, j):
    return jnp.broadcast_to(x[:, j:j + 1], x.shape)


def row(x, i):
    return jnp.broadcast_to(x[i:i + 1, :], x.shape)


def total_of(terms):
    while len(terms) > 1:
        terms = [x + y for x, y in zip(terms[::2], terms[1::2])] + terms[len(terms) & ~1:]
    return terms[0]


def small_factor(columns):
    a = {(i, j): row(columns[j], i) for j in range(SUB) for i in range(j, SUB)}
    factor, inverse = {}, {}
    for j in range(SUB):
        root = lax.rsqrt(a[j, j])
        inverse[j, j] = root
        for i in range(j + 1, SUB):
            factor[i, j] = a[i, j] * root
        for k in range(j + 1, SUB):
            for i in range(k, SUB):
                a[i, k] = a[i, k] - factor[i, j] * factor[k, j]
        for k in range(j):
            terms = [factor[j, i] * inverse[i, k] for i in range(k, j)]
            inverse[j, k] = total_of(terms) * -root
    return inverse


def inverse_factor(block):
    strips = NB // SUB
    left = [block[SUB * t:SUB * (t + 1), :] for t in range(strips)]
    rows = lax.broadcasted_iota(jnp.int32, (SUB, NB), 0)
    lanes = lax.broadcasted_iota(jnp.int32, (SUB, NB), 1)
    right = [jnp.where(lanes == rows + SUB * t, 1.0, 0.0) for t in range(strips)]
    done = []
    columns = [lane(left[0], j) for j in range(SUB)]
    for s in range(strips):
        inverse = small_factor(columns)
        factors = {}
        for t in range(s + 1, strips):
            old = [lane(left[t], SUB * s + j) for j in range(SUB)]
            factors[t] = [
                total_of([old[m] * inverse[j, m] for m in range(j + 1)]) for j in range(SUB)
            ]
            if t == s + 1:
                ahead = [lane(left[t], SUB * t + j) for j in range(SUB)]
                columns = [
                    ahead[j] - total_of([x * row(x, j) for x in factors[t]]) for j in range(SUB)
                ]
        upper_rows = [row(left[s], j) for j in range(SUB)]
        solved_rows = [row(right[s], j) for j in range(SUB)]
        spread = []
        for j in range(SUB):
            column = jnp.where(rows == j, inverse[j, j], 0.0)
            for i in range(j + 1, SUB):
                column = jnp.where(rows == i, inverse[i, j], column)
            spread.append(column)
        upper = total_of([x * y for x, y in zip(spread, upper_rows)])
        solved = total_of([x * y for x, y in zip(spread, solved_rows)])
        done.append(solved)
        upper_rows = [row(upper, j) for j in range(SUB)]
        solved_rows = [row(solved, j) for j in range(SUB)]
        for t in range(s + 1, strips):
            left[t] = left[t] - total_of([x * y for x, y in zip(factors[t], upper_rows)])
            right[t] = right[t] - total_of([x * y for x, y in zip(factors[t], solved_rows)])
    return jnp.concatenate(done, axis=0)


def eliminate(gram_ref, field_ref, low, done, total_ref, steps):
    for ref in (*low, *done):
        ref[...] = jnp.zeros_like(ref)

    def step(k, carry):
        here = pl.ds(pl.multiple_of(k * NB, NB), NB)
        mine = (low[0][here, :], low[1][here, :])
        block = gram_ref[here, here] - dot3(mine, mine, NT)
        inverse = split(inverse_factor(block))
        column = gram_ref[:, here] - dot3((low[0][...], low[1][...]), mine, NT)
        field = field_ref[here, :] - dot3(mine, (done[0][...], done[1][...]), NN)
        low[0][:, here], low[1][:, here] = split(dot3(split(column), inverse, NT))
        solved = dot3(inverse, split(field), NN)
        total_ref[here, :] = solved
        done[0][here, :], done[1][here, :] = split(solved)
        return carry

    lax.fori_loop(0, steps, step, 0)


def elimination_scratch(size, columns):
    shapes = ((size, size), (size, columns))
    return [pltpu.VMEM(shape, jnp.bfloat16) for shape in shapes for part in range(2)]


def factor_kernel(scale, place_ref, gram_ref, field_ref, out_ref, low0, low1, done0, done1, total):
    width = out_ref.shape[0]
    place = place_ref[0]
    steps = ((place + 1) * width + NB - 1) // NB
    eliminate(gram_ref, field_ref, (low0, low1), (done0, done1), total, steps)
    out_ref[...] = total[pl.ds(pl.multiple_of(place * width, SUB), width), :] * scale


def factor_and_solve(gram, field, place, width, scale):
    size, columns = field.shape
    return pl.pallas_call(
        functools.partial(factor_kernel, scale),
        out_shape=jax.ShapeDtypeStruct((width, columns), jnp.float32),
        in_specs=[SCALARS, WHOLE, WHOLE],
        out_specs=WHOLE,
        scratch_shapes=elimination_scratch(size, columns)
        + [pltpu.VMEM((size, columns), jnp.float32)],
        compiler_params=ROOMY,
        name="factor_and_solve",
    )(place, gram, field)


def joined(refs):
    return jnp.concatenate([ref[...] for ref in refs], axis=0)


def scatter_order(start, rows):
    quarter = start // (rows // 4)
    return ((quarter % 2) * 2 + quarter // 2 - quarter) * (rows // 4) + start


def own_gram_kernel(*refs):
    field, out_ref = joined(refs[:-1]), refs[-1]
    high, low = split(field)
    rows, unit = out_ref.shape[0], NB // 2
    for i in range(field.shape[0] // NB):
        here = slice(i * NB, (i + 1) * NB)
        end = (i + 1) * NB
        product = dot3((high[here], low[here]), (high[:end], low[:end]), NT)
        for j in range(i + 1):
            for part in range(0, NB, unit):
                start = scatter_order((i * (i + 1) // 2 + j) * NB + part, rows)
                out_ref[start:start + unit, :] = product[part:part + unit, j * NB:(j + 1) * NB]


def own_gram(field):
    blocks = sum(part.shape[0] for part in field) // NB
    rows = blocks * (blocks + 1) // 2 * NB
    return pl.pallas_call(
        own_gram_kernel,
        out_shape=jax.ShapeDtypeStruct((rows, NB), jnp.float32),
        in_specs=[WHOLE] * len(field),
        out_specs=WHOLE,
        compiler_params=ROOMY,
        name="own_gram",
    )(*field)


def cross_gram_kernel(*refs):
    half = (len(refs) - 1) // 2
    out_ref = refs[-1]
    mine, other = split(joined(refs[:half])), split(joined(refs[half:-1]))
    blocks = mine[0].shape[0] // NB
    for i in range(blocks):
        here = slice(i * NB, (i + 1) * NB)
        product = dot3((mine[0][here], mine[1][here]), other, NT)
        for j in range(blocks):
            start = (i * blocks + j) * NB
            out_ref[start:start + NB, :] = product[:, j * NB:(j + 1) * NB]


def cross_gram(field, other):
    size = sum(part.shape[0] for part in field)
    return pl.pallas_call(
        cross_gram_kernel,
        out_shape=jax.ShapeDtypeStruct((size * size // NB, NB), jnp.float32),
        in_specs=[WHOLE] * (2 * len(field)),
        out_specs=WHOLE,
        compiler_params=ROOMY,
        name="cross_gram",
    )(*field, *other)


def fetch(pairs, sems):
    copies = [pltpu.make_async_copy(x, y, sems.at[i]) for i, (x, y) in enumerate(pairs)]
    for copy in copies:
        copy.start()
    for copy in copies:
        copy.wait()


def rows_of(ref, start, rows):
    return ref.at[pl.ds(pl.multiple_of(start, SUB), rows), :]


def stacked(parts, target, columns):
    rows = parts[0].shape[0]
    return [(part, target.at[i * rows:(i + 1) * rows, :columns]) for i, part in enumerate(parts)]


def lower_blocks(flat, gram_ref):
    blocks = gram_ref.shape[0] // NB
    for i in range(blocks):
        for j in range(blocks):
            place = i * (i + 1) // 2 + j
            block = flat[place * NB:(place + 1) * NB, :] if j <= i else jnp.zeros((NB, NB), jnp.float32)
            gram_ref[i * NB:(i + 1) * NB, j * NB:(j + 1) * NB] = block


def first_half_kernel(where_ref, gram_in, *refs):
    mine, other = refs[:CHUNKS], refs[CHUNKS:2 * CHUNKS]
    top_ref, inverse_ref, flat, gram, field, total, low0, low1, done0, done1, sems = refs[2 * CHUNKS:]
    size, columns = top_ref.shape
    place, far = where_ref[0], where_ref[1]
    rows = gram_in.shape[2]
    pairs = [
        (gram_in.at[i, j], rows_of(flat, (i * 4 + (far ^ j)) * rows, rows))
        for i in range(4) for j in range(4)
    ]

    @pl.when(place == 0)
    def _():
        fetch(pairs + stacked(mine, field, columns), sems)

    @pl.when(place != 0)
    def _():
        fetch(pairs + stacked(other, field, columns), sems)

    lower_blocks(flat, gram)
    rows = lax.broadcasted_iota(jnp.int32, (size, size), 0)
    lanes = lax.broadcasted_iota(jnp.int32, (size, size), 1)
    field[:, columns:] = jnp.where(rows == lanes, 1.0, 0.0)
    eliminate(gram, field, (low0, low1), (done0, done1), total, size // NB)
    fetch([(total.at[:, :columns], top_ref), (total.at[:, columns:], inverse_ref)], sems)


def first_half(where, gram, mine, other):
    size, columns = sum(part.shape[0] for part in mine), mine[0].shape[1]
    f32 = jnp.float32
    return pl.pallas_call(
        first_half_kernel,
        out_shape=tuple(jax.ShapeDtypeStruct((size, n), f32) for n in (columns, size)),
        in_specs=[SCALARS] + [AFAR] * (1 + 2 * CHUNKS),
        out_specs=(AFAR, AFAR),
        scratch_shapes=[
            pltpu.VMEM((16 * gram.shape[2], NB), f32),
            pltpu.VMEM((size, size), f32),
            pltpu.VMEM((size, columns + size), f32),
            pltpu.VMEM((size, columns + size), f32),
        ] + elimination_scratch(size, columns + size) + [pltpu.SemaphoreType.DMA((16 + CHUNKS,))],
        compiler_params=ALONE,
        cost_estimate=pl.CostEstimate(flops=2 * 10 ** 10, bytes_accessed=10 ** 7, transcendentals=0),
        name="first_half",
    )(where, gram, *mine, *other)


def second_half_kernel(scale, where_ref, rest, *refs):
    mine = refs[:CHUNKS]
    top_in, inverse_in, out_ref = refs[CHUNKS:3 + CHUNKS]
    flat, corner, gram, top, inverse, field, total, low0, low1, done0, done1, sems = refs[3 + CHUNKS:]
    size, columns = top.shape
    blocks = size // NB
    rows = flat.shape[0] // 16

    @pl.when(where_ref[0] == 0)
    def _():
        fetch([(top_in, top)], sems)
        out_ref[...] = top[...] * scale

    @pl.when(where_ref[0] != 0)
    def _():
        pairs = stacked(mine, field, columns) + [(top_in, top), (inverse_in, inverse)]
        far = where_ref[1]
        for i in range(blocks):
            for j in range(blocks):
                here = far ^ j
                pairs.append((rest.at[i, j, :rows], rows_of(flat, (i * blocks + here) * rows, rows)))
                lanes = pl.ds(pl.multiple_of(here * NB, NB), NB)
                pairs.append((rest.at[i, j, rows:], corner.at[i * NB:(i + 1) * NB, lanes]))
        fetch(pairs, sems)
        lower_blocks(flat, gram)
        low = split(dot3(split(corner[...]), split(inverse[...]), NT))
        gram[...] = gram[...] - dot3(low, low, NT)
        field[...] = field[...] - dot3(low, split(top[...]), NN)
        eliminate(gram, field, (low0, low1), (done0, done1), total, blocks)
        out_ref[...] = total[...] * scale


def second_half(where, rest, mine, top, inverse, scale):
    size, columns = top.shape
    f32 = jnp.float32
    square, wide = pltpu.VMEM((size, size), f32), pltpu.VMEM((size, columns), f32)
    return pl.pallas_call(
        functools.partial(second_half_kernel, scale),
        out_shape=jax.ShapeDtypeStruct((size, columns), f32),
        in_specs=[SCALARS] + [AFAR] * (3 + CHUNKS),
        out_specs=WHOLE,
        scratch_shapes=[
            pltpu.VMEM((16 * (rest.shape[2] - NB), NB), f32), square, square, wide, square, wide, wide,
        ] + elimination_scratch(size, columns) + [pltpu.SemaphoreType.DMA((34 + CHUNKS,))],
        compiler_params=ALONE,
        name="second_half",
    )(where, rest, *mine, top, inverse)


NEAR, FAR = 1, 4


def send(x, stride, planes=None):
    devices, sides = lax.axis_size("rows"), lax.axis_size("vecs")
    pairs = [
        (i * sides + v, (i ^ stride) * sides + v)
        for i in range(devices) for v in (range(sides) if planes is None else planes)
    ]
    return lax.ppermute(x, ("rows", "vecs"), pairs)


def send_up(x, stride):
    devices, sides = lax.axis_size("rows"), lax.axis_size("vecs")
    pairs = [(i * sides, (i ^ stride) * sides + 1) for i in range(devices)]
    return lax.ppermute(x, ("rows", "vecs"), pairs)


def swap_half(x, bit, stride, planes=None):
    halves = x.reshape(2, -1, NB)
    kept = lax.dynamic_index_in_dim(halves, bit, 0, keepdims=False)
    given = lax.dynamic_index_in_dim(halves, 1 - bit, 0, keepdims=False)
    return kept + send(given, stride, planes)


def reduce_group(x, here, stride, planes=None):
    parts = x.reshape(4, -1, NB)
    total = lax.dynamic_index_in_dim(parts, here, 0, keepdims=False)
    others = [
        send(lax.dynamic_index_in_dim(parts, here ^ i, 0, keepdims=False), i * stride, planes)
        for i in range(1, 4)
    ]
    return total + others[0] + (others[1] + others[2])


def orthonormalize_planes(current, scale):
    together = lax.optimization_barrier
    rank = lax.axis_index("rows")
    place = lax.axis_index("vecs")
    near, far = rank % 4, rank // 4
    where = jnp.stack([place, far]).astype(jnp.int32)
    near_groups = [list(range(4 * g, 4 * g + 4)) for g in range(4)]
    far_groups = [list(range(g, 16, 4)) for g in range(4)]
    below = [send_up(part, 0) for part in current]
    half = swap_half(own_gram(current), near % 2, 1)
    half, below[0] = together((half, below[0]))
    fourth = swap_half(half, near // 2, 2)
    fourth, *below = together((fourth, *below))
    fourth, corner = together((fourth, cross_gram(current, below)))
    corner = lax.psum_scatter(corner, "rows", axis_index_groups=near_groups, tiled=True)
    mine = reduce_group(fourth, far, FAR)
    first = jnp.where(place == 0, mine, send_up(mine, 0))
    first = jnp.stack([first] + [send(first, i * FAR) for i in range(1, 4)])
    first, corner = together((first, corner))
    gram = lax.all_gather(first, "rows", axis_index_groups=near_groups)
    corner = lax.all_to_all(corner.reshape(4, -1, NB), "rows", 0, 0, axis_index_groups=far_groups)
    corner = jnp.sum(corner, axis=0)
    rest = jnp.concatenate([mine, corner], axis=0)
    rest = jnp.stack([rest] + [send(rest, i * FAR, (1,)) for i in range(1, 4)])
    gram, rest = together((gram, rest))
    rest = lax.all_gather(rest, "rows", axis_index_groups=near_groups)
    top, inverse = first_half(where, gram, current, below)
    return second_half(where, rest, current, top, inverse, scale)


def orthonormalize(current, scale):
    current = jnp.concatenate(current, axis=0)
    width = current.shape[0]
    gathered = lax.all_gather(current, "vecs", axis=0, tiled=True)
    partial_rows = jnp.einsum("mn,kn->mk", current, gathered, precision=lax.Precision.HIGHEST)
    summed_rows = lax.psum(partial_rows, "rows")
    gram = lax.all_gather(summed_rows, "vecs", axis=0, tiled=True)
    place = lax.axis_index("vecs").astype(jnp.int32)[None]
    return factor_and_solve(gram, gathered, place, width, scale)


def body(tiles, columns, start_vectors):
    blocks_here = tiles.shape[0]
    total_blocks = blocks_here * lax.axis_size("rows")
    first_block = lax.axis_index("rows") * blocks_here
    global_rows = first_block + jnp.arange(blocks_here, dtype=jnp.int32)
    offsets = jnp.mod(columns - global_rows[:, None] + HB, total_blocks)
    slots = jnp.arange(blocks_here, dtype=jnp.int32)[:, None] + offsets
    current = chebyshev(tiles, slots, start_vectors)
    scale = float((total_blocks * BS) ** 0.5)
    fits = (
        lax.axis_size("vecs") == 2
        and lax.axis_size("rows") == 16
        and start_vectors.shape[0] == 4 * NB
    )
    return (orthonormalize_planes if fits else orthonormalize)(current, scale)


def solution(mesh):
    placed = (P("rows", None, None, None), P("rows", None), P("vecs", "rows"))
    return jax.shard_map(
        body, mesh=mesh, in_specs=placed, out_specs=P("vecs", "rows"), check_vma=False
    )
```

```python
import functools

import jax
import jax.numpy as jnp
from jax import lax
from jax.experimental import pallas as pl
from jax.experimental.pallas import tpu as pltpu
from jax.sharding import PartitionSpec as P

BS = 128
HB = 3
STEPS = 4
NB = 128
SUB = 8
CHUNKS = 2
NT = (((1,), (1,)), ((), ()))
NN = (((1,), (0,)), ((), ()))
SCALARS = pl.BlockSpec(memory_space=pltpu.SMEM)
WHOLE = pl.BlockSpec(memory_space=pltpu.VMEM)
AFAR = pl.BlockSpec(memory_space=pl.ANY)
ROOMY = pltpu.CompilerParams(vmem_limit_bytes=28 * 2 ** 20)
ALONE = pltpu.CompilerParams(vmem_limit_bytes=48 * 2 ** 20)


def split(x):
    high = x.astype(jnp.bfloat16)
    return high, (x - high.astype(jnp.float32)).astype(jnp.bfloat16)


def dot3(a, b, dims):
    def dot(x, y):
        return lax.dot_general(x, y, dims, preferred_element_type=jnp.float32)

    return dot(a[0], b[0]) + (dot(a[0], b[1]) + dot(a[1], b[0]))


def band_kernel(slots_ref, tiles_ref, band_ref):
    band_ref[...] = jnp.zeros_like(band_ref)
    for b in range(tiles_ref.shape[0]):
        for t in range(tiles_ref.shape[1]):
            start = pl.multiple_of(slots_ref[b, t] * BS, BS)
            flipped = tiles_ref[b, t].astype(jnp.float32).T
            band_ref[pl.ds(start, BS), b * BS:(b + 1) * BS] = flipped.astype(jnp.bfloat16)


def band_matrix(tiles, slots):
    blocks = tiles.shape[0]
    return pl.pallas_call(
        band_kernel,
        out_shape=jax.ShapeDtypeStruct(((blocks + 2 * HB) * BS, blocks * BS), jnp.bfloat16),
        in_specs=[SCALARS, WHOLE],
        out_specs=WHOLE,
        compiler_params=ROOMY,
        name="band_matrix",
    )(slots, tiles)


def step_kernel(has_previous, has_edges, *refs):
    before_ref, current_ref, after_ref, band_ref = refs[:4]
    outs = refs[4 + has_previous:]
    parts = [ref[...] for ref in (before_ref, current_ref, after_ref)]
    highs, lows = zip(*[split(part) for part in parts])
    high, low = jnp.concatenate(highs, axis=1), jnp.concatenate(lows, axis=1)
    columns = current_ref.shape[1]
    blocks = columns // BS
    halo = HB * BS
    for b in range(0, blocks, 2):
        end = min(b + 2, blocks)
        here = slice(b * BS, end * BS)
        depth = slice(b * BS, (end + 2 * HB) * BS)
        band = band_ref[depth, here]

        def dot(x):
            return jnp.dot(x[:, depth], band, preferred_element_type=jnp.float32)

        result = dot(high) + dot(low)
        if has_previous:
            result = 2.0 * result - refs[4][:, here]
        outs[0][:, here] = result
    if has_edges:
        outs[1][...] = outs[0][:, columns - halo:]
        outs[2][...] = outs[0][:, :halo]


def filter_step(halos, current, band, previous, has_edges):
    before, after = halos
    width, columns = current.shape
    f32 = jnp.float32
    edge = jax.ShapeDtypeStruct((width, HB * BS), f32)
    shapes = (jax.ShapeDtypeStruct((width, columns), f32),) + (edge, edge) * has_edges
    operands = (before, current, after, band) + ((previous,) if previous is not None else ())
    return pl.pallas_call(
        functools.partial(step_kernel, previous is not None, has_edges),
        out_shape=shapes,
        in_specs=[WHOLE] * len(operands),
        out_specs=(WHOLE,) * len(shapes),
        compiler_params=ROOMY,
        cost_estimate=pl.CostEstimate(
            flops=4 * width * columns * (2 + 2 * HB) * BS,
            bytes_accessed=4 * width * columns * 6,
            transcendentals=0,
        ),
        name="filter_step",
    )(*operands)


def exchange_edges(last, first):
    devices = lax.axis_size("rows")
    up = [(i, (i + 1) % devices) for i in range(devices)]
    down = [(j, i) for i, j in up]
    return lax.ppermute(last, "rows", up), lax.ppermute(first, "rows", down)


def chebyshev(tiles, slots, start_vectors):
    rows = start_vectors.shape[0] // CHUNKS
    halo = HB * BS
    current = [start_vectors[c * rows:(c + 1) * rows] for c in range(CHUNKS)]
    previous = [None] * CHUNKS
    halos = [exchange_edges(x[:, x.shape[1] - halo:], x[:, :halo]) for x in current]
    band = band_matrix(tiles, slots)
    for step in range(STEPS):
        more = step < STEPS - 1
        for c in range(CHUNKS):
            halos[c], current[c - 1] = lax.optimization_barrier((halos[c], current[c - 1]))
            following, *edges = filter_step(halos[c], current[c], band, previous[c], more)
            previous[c], current[c] = current[c], following
            if more:
                halos[c] = exchange_edges(*edges)
    return current


def lane(x, j):
    return jnp.broadcast_to(x[:, j:j + 1], x.shape)


def row(x, i):
    return jnp.broadcast_to(x[i:i + 1, :], x.shape)


def total_of(terms):
    while len(terms) > 1:
        terms = [x + y for x, y in zip(terms[::2], terms[1::2])] + terms[len(terms) & ~1:]
    return terms[0]


def small_factor(columns):
    a = {(i, j): row(columns[j], i) for j in range(SUB) for i in range(j, SUB)}
    factor, inverse = {}, {}
    for j in range(SUB):
        root = lax.rsqrt(a[j, j])
        inverse[j, j] = root
        for i in range(j + 1, SUB):
            factor[i, j] = a[i, j] * root
        for k in range(j + 1, SUB):
            for i in range(k, SUB):
                a[i, k] = a[i, k] - factor[i, j] * factor[k, j]
        for k in range(j):
            terms = [factor[j, i] * inverse[i, k] for i in range(k, j)]
            inverse[j, k] = total_of(terms) * -root
    return inverse


def inverse_factor(block):
    strips = NB // SUB
    left = [block[SUB * t:SUB * (t + 1), :] for t in range(strips)]
    rows = lax.broadcasted_iota(jnp.int32, (SUB, NB), 0)
    lanes = lax.broadcasted_iota(jnp.int32, (SUB, NB), 1)
    right = [jnp.where(lanes == rows + SUB * t, 1.0, 0.0) for t in range(strips)]
    done = []
    columns = [lane(left[0], j) for j in range(SUB)]
    for s in range(strips):
        inverse = small_factor(columns)
        factors = {}
        if s + 1 < strips:
            t = s + 1
            old = [lane(left[t], SUB * s + j) for j in range(SUB)]
            factors[t] = [
                total_of([old[m] * inverse[j, m] for m in range(j + 1)]) for j in range(SUB)
            ]
            ahead = [lane(left[t], SUB * t + j) for j in range(SUB)]
            columns = [
                ahead[j] - total_of([x * row(x, j) for x in factors[t]]) for j in range(SUB)
            ]
        upper_rows = [row(left[s], j) for j in range(SUB)]
        solved_rows = [row(right[s], j) for j in range(SUB)]
        spread = []
        for j in range(SUB):
            column = jnp.where(rows == j, inverse[j, j], 0.0)
            for i in range(j + 1, SUB):
                column = jnp.where(rows == i, inverse[i, j], column)
            spread.append(column)
        upper = total_of([x * y for x, y in zip(spread, upper_rows)])
        solved = total_of([x * y for x, y in zip(spread, solved_rows)])
        done.append(solved)
        upper_rows = [row(upper, j) for j in range(SUB)]
        solved_rows = [row(solved, j) for j in range(SUB)]
        if s + 2 < strips:
            turned = upper.T
            for t in range(s + 2, strips):
                strip = turned[SUB * t:SUB * (t + 1), :]
                factors[t] = [
                    jnp.broadcast_to(strip[:, j:j + 1], (SUB, NB)) for j in range(SUB)
                ]
        for t in range(s + 1, strips):
            left[t] = left[t] - total_of([x * y for x, y in zip(factors[t], upper_rows)])
            right[t] = right[t] - total_of([x * y for x, y in zip(factors[t], solved_rows)])
    return jnp.concatenate(done, axis=0)


def eliminate(gram_ref, field_ref, low, done, total_ref, steps):
    for ref in (*low, *done):
        ref[...] = jnp.zeros_like(ref)

    def step(k, carry):
        here = pl.ds(pl.multiple_of(k * NB, NB), NB)
        mine = (low[0][here, :], low[1][here, :])
        block = gram_ref[here, here] - dot3(mine, mine, NT)
        inverse = split(inverse_factor(block))
        column = gram_ref[:, here] - dot3((low[0][...], low[1][...]), mine, NT)
        field = field_ref[here, :] - dot3(mine, (done[0][...], done[1][...]), NN)
        low[0][:, here], low[1][:, here] = split(dot3(split(column), inverse, NT))
        solved = dot3(inverse, split(field), NN)
        total_ref[here, :] = solved
        done[0][here, :], done[1][here, :] = split(solved)
        return carry

    lax.fori_loop(0, steps, step, 0)


def elimination_scratch(size, columns):
    shapes = ((size, size), (size, columns))
    return [pltpu.VMEM(shape, jnp.bfloat16) for shape in shapes for part in range(2)]


def factor_kernel(scale, place_ref, gram_ref, field_ref, out_ref, low0, low1, done0, done1, total):
    width = out_ref.shape[0]
    place = place_ref[0]
    steps = ((place + 1) * width + NB - 1) // NB
    eliminate(gram_ref, field_ref, (low0, low1), (done0, done1), total, steps)
    out_ref[...] = total[pl.ds(pl.multiple_of(place * width, SUB), width), :] * scale


def factor_and_solve(gram, field, place, width, scale):
    size, columns = field.shape
    return pl.pallas_call(
        functools.partial(factor_kernel, scale),
        out_shape=jax.ShapeDtypeStruct((width, columns), jnp.float32),
        in_specs=[SCALARS, WHOLE, WHOLE],
        out_specs=WHOLE,
        scratch_shapes=elimination_scratch(size, columns)
        + [pltpu.VMEM((size, columns), jnp.float32)],
        compiler_params=ROOMY,
        name="factor_and_solve",
    )(place, gram, field)


def joined(refs):
    return jnp.concatenate([ref[...] for ref in refs], axis=0)


def scatter_order(start, rows):
    quarter = start // (rows // 4)
    return ((quarter % 2) * 2 + quarter // 2 - quarter) * (rows // 4) + start


def own_gram_kernel(*refs):
    field, out_ref = joined(refs[:-1]), refs[-1]
    high, low = split(field)
    rows, unit = out_ref.shape[0], NB // 2
    for i in range(field.shape[0] // NB):
        here = slice(i * NB, (i + 1) * NB)
        end = (i + 1) * NB
        product = dot3((high[here], low[here]), (high[:end], low[:end]), NT)
        for j in range(i + 1):
            for part in range(0, NB, unit):
                start = scatter_order((i * (i + 1) // 2 + j) * NB + part, rows)
                out_ref[start:start + unit, :] = product[part:part + unit, j * NB:(j + 1) * NB]


def own_gram(field):
    blocks = sum(part.shape[0] for part in field) // NB
    rows = blocks * (blocks + 1) // 2 * NB
    return pl.pallas_call(
        own_gram_kernel,
        out_shape=jax.ShapeDtypeStruct((rows, NB), jnp.float32),
        in_specs=[WHOLE] * len(field),
        out_specs=WHOLE,
        compiler_params=ROOMY,
        name="own_gram",
    )(*field)


def cross_gram_kernel(*refs):
    half = (len(refs) - 1) // 2
    out_ref = refs[-1]
    mine, other = split(joined(refs[:half])), split(joined(refs[half:-1]))
    rows = out_ref.shape[0]
    blocks = mine[0].shape[0] // NB
    for i in range(blocks):
        here = slice(i * NB, (i + 1) * NB)
        product = dot3((mine[0][here], mine[1][here]), other, NT)
        for j in range(blocks):
            start = scatter_order((i * blocks + j) * NB, rows)
            out_ref[start:start + NB, :] = product[:, j * NB:(j + 1) * NB]


def cross_gram(field, other):
    size = sum(part.shape[0] for part in field)
    return pl.pallas_call(
        cross_gram_kernel,
        out_shape=jax.ShapeDtypeStruct((size * size // NB, NB), jnp.float32),
        in_specs=[WHOLE] * (2 * len(field)),
        out_specs=WHOLE,
        compiler_params=ROOMY,
        name="cross_gram",
    )(*field, *other)


def fetch(pairs, sems):
    copies = [pltpu.make_async_copy(x, y, sems.at[i]) for i, (x, y) in enumerate(pairs)]
    for copy in copies:
        copy.start()
    for copy in copies:
        copy.wait()


def rows_of(ref, start, rows):
    return ref.at[pl.ds(pl.multiple_of(start, SUB), rows), :]


def stacked(parts, target, columns):
    rows = parts[0].shape[0]
    return [(part, target.at[i * rows:(i + 1) * rows, :columns]) for i, part in enumerate(parts)]


def lower_blocks(flat, gram_ref, first):
    blocks = gram_ref.shape[0] // NB
    for i in range(blocks):
        for j in range(blocks):
            place = (first + i) * (first + i + 1) // 2 + first + j
            block = flat[place * NB:(place + 1) * NB, :] if j <= i else jnp.zeros((NB, NB), jnp.float32)
            gram_ref[i * NB:(i + 1) * NB, j * NB:(j + 1) * NB] = block


def inverted(low, first, second):
    return -dot3(split(second), split(dot3(low, first, NN)), NN)


def identity(size):
    rows = lax.broadcasted_iota(jnp.int32, (size, size), 0)
    lanes = lax.broadcasted_iota(jnp.int32, (size, size), 1)
    return jnp.where(rows == lanes, 1.0, 0.0)


def first_quarter_kernel(where_ref, *refs):
    pieces, mine, other, top_ref, inverse_ref = refs[:4], refs[4], refs[5], refs[6], refs[7]
    flat, gram, field, total, low0, low1, done0, done1, sems = refs[8:]
    place, near, far = where_ref[0], where_ref[1], where_ref[2]
    size, columns = top_ref.shape
    rows = pieces[0].shape[1]
    pairs = [
        (piece.at[j], rows_of(flat, ((near ^ i) * 4 + (far ^ j)) * rows, rows))
        for i, piece in enumerate(pieces) for j in range(4)
    ]

    @pl.when(place == 0)
    def _():
        fetch(pairs + stacked([mine], field, columns), sems)

    @pl.when(place != 0)
    def _():
        fetch(pairs + stacked([other], field, columns), sems)

    lower_blocks(flat, gram, 0)
    field[:, columns:] = identity(size)
    eliminate(gram, field, (low0, low1), (done0, done1), total, size // NB)
    fetch([(total.at[:, :columns], top_ref), (total.at[:, columns:], inverse_ref)], sems)


def second_quarter_kernel(where_ref, *refs):
    pieces, mine, other, top_in, inverse_in, top_ref, inverse_ref = refs[:4], *refs[4:10]
    flat, gram, corner, top, inverse, field, total, low0, low1, done0, done1, sems = refs[10:]
    place, near, far = where_ref[0], where_ref[1], where_ref[2]
    size, columns = mine.shape
    rows = pieces[0].shape[1]
    pairs = [
        (piece.at[j], rows_of(flat, ((near ^ i) * 4 + (far ^ j)) * rows, rows))
        for i, piece in enumerate(pieces) for j in range(4)
    ] + [(top_in, top), (inverse_in, inverse)]

    @pl.when(place == 0)
    def _():
        fetch(pairs + stacked([mine], field, columns), sems)

    @pl.when(place != 0)
    def _():
        fetch(pairs + stacked([other], field, columns), sems)

    blocks = size // NB
    lower_blocks(flat, gram, blocks)
    for i in range(blocks):
        for j in range(blocks):
            start = ((blocks + i) * (blocks + i + 1) // 2 + j) * NB
            corner[i * NB:(i + 1) * NB, j * NB:(j + 1) * NB] = flat[start:start + NB, :]
    first = split(inverse[...])
    low = split(dot3(split(corner[...]), first, NT))
    gram[...] = gram[...] - dot3(low, low, NT)
    field[:, :columns] = field[:, :columns] - dot3(low, split(top[...]), NN)
    field[:, columns:] = identity(size)
    eliminate(gram, field, (low0, low1), (done0, done1), total, blocks)
    corner[...] = inverted(low, first, total[:, columns:])
    gram[...] = jnp.zeros_like(gram)
    fetch([
        (top, top_ref.at[:size]),
        (total.at[:, :columns], top_ref.at[size:]),
        (inverse, inverse_ref.at[:size, :size]),
        (gram, inverse_ref.at[:size, size:]),
        (corner, inverse_ref.at[size:, :size]),
        (total.at[:, columns:], inverse_ref.at[size:, size:]),
    ], sems)


def quarter(kernel, where, pieces, mine, other, *before):
    size, columns = mine.shape
    f32 = jnp.float32
    flat_rows = 4 * pieces[0].shape[0] * pieces[0].shape[1]
    operands = (*pieces, mine, other, *before)
    results = 2 * size if before else size
    square, wide = pltpu.VMEM((size, size), f32), pltpu.VMEM((size, columns + size), f32)
    earlier = [square, pltpu.VMEM((size, columns), f32), square] if before else []
    return pl.pallas_call(
        kernel,
        out_shape=tuple(jax.ShapeDtypeStruct((results, n), f32) for n in (columns, results)),
        in_specs=[SCALARS] + [AFAR] * len(operands),
        out_specs=(AFAR, AFAR),
        scratch_shapes=[pltpu.VMEM((flat_rows, NB), f32), square] + earlier + [wide, wide]
        + elimination_scratch(size, columns + size) + [pltpu.SemaphoreType.DMA((19,))],
        compiler_params=ALONE,
        cost_estimate=pl.CostEstimate(flops=10 ** 10, bytes_accessed=10 ** 7, transcendentals=0),
        name="second_quarter" if before else "first_quarter",
    )(where, *operands)


def second_half_kernel(scale, where_ref, *refs):
    pieces, corners, mine = refs[0], refs[1:5], refs[5:5 + CHUNKS]
    top_in, inverse_in, out_ref = refs[5 + CHUNKS:8 + CHUNKS]
    flat, corner, gram, top, inverse, field, total, low0, low1, done0, done1, sems = refs[8 + CHUNKS:]
    place, near, far = where_ref[0], where_ref[1], where_ref[2]
    size, columns = top.shape
    blocks = size // NB
    rows = pieces.shape[2]

    @pl.when(place == 0)
    def _():
        fetch([(top_in, top)], sems)
        out_ref[...] = top[...] * scale

    @pl.when(place != 0)
    def _():
        pairs = stacked(mine, field, columns) + [(top_in, top), (inverse_in, inverse)]
        for i in range(4):
            for j in range(4):
                pairs.append((pieces.at[i, j], rows_of(flat, (i * 4 + (far ^ j)) * rows, rows)))
                lanes = pl.ds(pl.multiple_of((far ^ j) * NB, NB), NB)
                target = corner.at[pl.ds(pl.multiple_of((near ^ i) * NB, NB), NB), lanes]
                pairs.append((corners[i].at[j], target))
        fetch(pairs, sems)
        lower_blocks(flat, gram, 0)
        low = split(dot3(split(corner[...]), split(inverse[...]), NT))
        gram[...] = gram[...] - dot3(low, low, NT)
        field[...] = field[...] - dot3(low, split(top[...]), NN)
        eliminate(gram, field, (low0, low1), (done0, done1), total, blocks)
        out_ref[...] = total[...] * scale


def second_half(where, pieces, corners, mine, top, inverse, scale):
    size, columns = top.shape
    f32 = jnp.float32
    square, wide = pltpu.VMEM((size, size), f32), pltpu.VMEM((size, columns), f32)
    return pl.pallas_call(
        functools.partial(second_half_kernel, scale),
        out_shape=jax.ShapeDtypeStruct((size, columns), f32),
        in_specs=[SCALARS] + [AFAR] * (7 + CHUNKS),
        out_specs=WHOLE,
        scratch_shapes=[
            pltpu.VMEM((16 * pieces.shape[2], NB), f32), square, square, wide, square, wide, wide,
        ] + elimination_scratch(size, columns) + [pltpu.SemaphoreType.DMA((34 + CHUNKS,))],
        compiler_params=ALONE,
        name="second_half",
    )(where, pieces, *corners, *mine, top, inverse)


NEAR, FAR = 1, 4


def send(x, stride, planes=None):
    devices, sides = lax.axis_size("rows"), lax.axis_size("vecs")
    pairs = [
        (i * sides + v, (i ^ stride) * sides + v)
        for i in range(devices) for v in (range(sides) if planes is None else planes)
    ]
    return lax.ppermute(x, ("rows", "vecs"), pairs)


def send_up(x, stride):
    devices, sides = lax.axis_size("rows"), lax.axis_size("vecs")
    pairs = [(i * sides, (i ^ stride) * sides + 1) for i in range(devices)]
    return lax.ppermute(x, ("rows", "vecs"), pairs)


def swap_half(x, bit, stride, planes=None):
    halves = x.reshape(2, -1, NB)
    kept = lax.dynamic_index_in_dim(halves, bit, 0, keepdims=False)
    given = lax.dynamic_index_in_dim(halves, 1 - bit, 0, keepdims=False)
    return kept + send(given, stride, planes)


def reduce_group(x, here, stride, planes=None):
    parts = x.reshape(4, -1, NB)
    total = lax.dynamic_index_in_dim(parts, here, 0, keepdims=False)
    others = [
        send(lax.dynamic_index_in_dim(parts, here ^ i, 0, keepdims=False), i * stride, planes)
        for i in range(1, 4)
    ]
    return total + others[0] + (others[1] + others[2])


def orthonormalize_planes(current, scale):
    together = lax.optimization_barrier
    rank = lax.axis_index("rows")
    place = lax.axis_index("vecs")
    near, far = rank % 4, rank // 4
    where = jnp.stack([place, near, far]).astype(jnp.int32)
    near_groups = [list(range(4 * g, 4 * g + 4)) for g in range(4)]
    below = [send_up(part, 0) for part in current]
    own, below[0] = together((current, below[0]))
    half = swap_half(own_gram(own), near % 2, 1)
    fourth = swap_half(half, near // 2, 2)
    mine = reduce_group(fourth, far, FAR)
    mine, *below = together((mine, *below))
    first = jnp.where(place == 0, mine, send_up(mine, 0))
    corner = swap_half(cross_gram(current, below), near % 2, 1, (1,))
    first, corner = together((first, corner))
    both = jnp.concatenate([first, mine], axis=0)
    both = jnp.stack([both] + [send(both, i * FAR) for i in range(1, 4)])
    corner = swap_half(corner, near // 2, 2, (1,))
    both, corner = together((both, corner))
    rows = mine.shape[0]
    first, second = both[:, :rows], both[:, rows:]
    second = lax.all_gather(second, "rows", axis_index_groups=near_groups)
    pieces = [first] + [send(first, i * NEAR) for i in range(1, 4)]
    corner = reduce_group(corner, far, FAR, (1,))
    pieces, corner = together((pieces, corner))
    top, inverse = quarter(first_quarter_kernel, where, pieces, current[0], below[0])
    corner = jnp.stack([corner] + [send(corner, i * FAR, (1,)) for i in range(1, 4)])
    top, inverse, corner = together((top, inverse, corner))
    top, inverse = quarter(second_quarter_kernel, where, pieces, current[1], below[1], top, inverse)
    corners = [corner] + [send(corner, i * NEAR, (1,)) for i in range(1, 4)]
    return second_half(where, second, corners, current, top, inverse, scale)


def orthonormalize(current, scale):
    current = jnp.concatenate(current, axis=0)
    width = current.shape[0]
    gathered = lax.all_gather(current, "vecs", axis=0, tiled=True)
    partial_rows = jnp.einsum("mn,kn->mk", current, gathered, precision=lax.Precision.HIGHEST)
    summed_rows = lax.psum(partial_rows, "rows")
    gram = lax.all_gather(summed_rows, "vecs", axis=0, tiled=True)
    place = lax.axis_index("vecs").astype(jnp.int32)[None]
    return factor_and_solve(gram, gathered, place, width, scale)


def body(tiles, columns, start_vectors):
    blocks_here = tiles.shape[0]
    total_blocks = blocks_here * lax.axis_size("rows")
    first_block = lax.axis_index("rows") * blocks_here
    global_rows = first_block + jnp.arange(blocks_here, dtype=jnp.int32)
    offsets = jnp.mod(columns - global_rows[:, None] + HB, total_blocks)
    slots = jnp.arange(blocks_here, dtype=jnp.int32)[:, None] + offsets
    current = chebyshev(tiles, slots, start_vectors)
    scale = float((total_blocks * BS) ** 0.5)
    fits = (
        lax.axis_size("vecs") == 2
        and lax.axis_size("rows") == 16
        and start_vectors.shape[0] == 4 * NB
    )
    return (orthonormalize_planes if fits else orthonormalize)(current, scale)


def solution(mesh):
    placed = (P("rows", None, None, None), P("rows", None), P("vecs", "rows"))
    return jax.shard_map(
        body, mesh=mesh, in_specs=placed, out_specs=P("vecs", "rows"), check_vma=False
    )
```
